32 devices in a mesh: cases: 2 (over x), azim: 16 (over z, y, core).
Axes of the slice: x: 2, y: 2, z: 4, core: 2. Of those that a mesh axis runs over, the one named last changes fastest.
Arguments:
- wake: float32 [3, 32, 32, 128], P(None, ('cases', 'azim')), parts along dimension 1
- release: float32 [3, 32, 128], P(None, ('cases', 'azim')), parts along dimension 1
- strength: float32 [32, 128], P(('cases', 'azim')), parts along dimension 0, may hold values from -6 to 6
- source_list: int32 [32, 32, 8], P(('cases', 'azim')), parts along dimension 0, may hold values from 0 to 511, as said below
- list_count: int32 [32, 32], P(('cases', 'azim')), parts along dimension 0, may hold values from 1 to 8, as said below
Outputs:
- relaxed: float32 [3, 32, 32, 128], P(None, ('cases', 'azim')), parts along dimension 1
- induced: float32 [3, 32, 32, 128], P(None, ('cases', 'azim')), parts along dimension 1
The draws below stay inside these ranges and needn't reach their ends.
There are 2 independent parts, one for each index of `cases`. The reference program is written for one: setup_inputs(seed, part) draws one part's arguments, and reference() takes and returns one part's arrays. A program takes and returns all parts, laid end to end along the dimension named above; each array names one. Nothing has to cross between parts.
Inputs may be any that keep to these rules, and one draw needn't show every extreme that they name: `source_list`: every listed tile lies in an azimuth block of 1 step that is -1 to 0 blocks, cyclically, from the target tile's block; slots at or past the tile's count hold valid ids too. `list_count`: some tile holds 8.
All inputs are finite; a program needn't handle non-finite values.
Results may differ from the reference program's by a relative error of at most 0.0001.
Values sent between devices are 32-bit elements; how exact they have to be, the bound alone decides.
A program may use at most 64 MiB of HBM per device.

```python
import math
import jax
import jax.numpy as jnp
from jax import lax

ROTORS = 2
BLADES = 4
TRAILERS = 16
PSI_DEV = 1
AGE = 32
LIST = 8
SWEEPS = 2
PSI = 16
REACH_DEV = 1


def helix_nodes(key, age_values, noise_scale):
    psi_index = jnp.arange(PSI, dtype=jnp.float32)[:, None, None]
    node_index = jnp.arange(ROTORS * BLADES * TRAILERS, dtype=jnp.int32)
    rotor_side = (node_index // (BLADES * TRAILERS)).astype(jnp.float32)
    blade_index = (node_index // TRAILERS % BLADES).astype(jnp.float32)
    trailer_index = (node_index % TRAILERS).astype(jnp.float32)
    turn_step = 2.0 * math.pi / PSI
    spin = 1.0 - 2.0 * rotor_side
    theta = spin * (psi_index - age_values) * turn_step + blade_index * (2.0 * math.pi / BLADES)
    radial = (0.25 + 0.75 * (trailer_index + 0.5) / TRAILERS) * (0.8 + 0.2 * jnp.exp(-age_values * turn_step))
    height = 0.15 * spin - 0.1 * age_values * turn_step + 0.0 * psi_index
    shape_all = (3, PSI, age_values.shape[1], ROTORS * BLADES * TRAILERS)
    jitter = jax.random.normal(key, shape_all, jnp.float32) * noise_scale
    radial = radial + 0.0 * theta
    return jnp.stack([radial * jnp.cos(theta), radial * jnp.sin(theta), height]) + jitter


def draw_wake(key, part):
    ages = jnp.arange(AGE, dtype=jnp.float32)[None, :, None]
    return helix_nodes(jax.random.fold_in(key, 11), ages, 0.1)


def draw_release(key, part):
    ages = jnp.zeros((1, 1, 1), jnp.float32)
    return helix_nodes(jax.random.fold_in(key, 12), ages, 0.2)[:, :, 0, :]


def draw_source_list(key, part):
    keys = jax.random.split(jax.random.fold_in(key, 21), 3)
    device_count = PSI // PSI_DEV
    owner_block = (jnp.arange(PSI, dtype=jnp.int32) // PSI_DEV)[:, None, None]
    offset = jax.random.randint(keys[0], (PSI, AGE, LIST), -REACH_DEV, REACH_DEV, dtype=jnp.int32)
    block_index = (owner_block + offset) % device_count
    column = block_index * PSI_DEV + jax.random.randint(keys[1], (PSI, AGE, LIST), 0, PSI_DEV, dtype=jnp.int32)
    age_pick = jax.random.randint(keys[2], (PSI, AGE, LIST), 0, AGE, dtype=jnp.int32)
    return (column * AGE + age_pick).astype(jnp.int32)


def draw_list_count(key, part):
    keys = jax.random.split(jax.random.fold_in(key, 31), 3)
    device_count = PSI // PSI_DEV
    band_start = jax.random.randint(keys[0], (), 0, device_count, dtype=jnp.int32)
    owner_block = (jnp.arange(PSI, dtype=jnp.int32) // PSI_DEV)[:, None]
    dense = (owner_block - band_start) % device_count < max(1, device_count // 4)
    higher = jax.random.randint(keys[1], (PSI, AGE), LIST // 2, LIST + 1, dtype=jnp.int32)
    lower = jax.random.randint(keys[2], (PSI, AGE), 1, LIST // 2 + 1, dtype=jnp.int32)
    counts = jnp.where(dense, higher, lower)
    peak = (jnp.arange(PSI, dtype=jnp.int32)[:, None] == band_start * PSI_DEV) & (jnp.arange(AGE, dtype=jnp.int32)[None, :] == 0)
    return jnp.where(peak, LIST, counts).astype(jnp.int32)


def block_scale(stream_key, dims, cuts, least, largest):
    gain, own = 1.0, jax.random.fold_in(stream_key, 6)
    for dim, shards_of in cuts:
        steps = jnp.exp(jax.random.uniform(jax.random.fold_in(own, dim), (shards_of,), jnp.float32, least / len(cuts), largest / len(cuts)))
        gain = gain * jnp.repeat(steps, dims[dim] // shards_of).reshape([-1 if axis == dim else 1 for axis in range(len(dims))])
    return gain


def gaussian(key, dims, spread, reach, shards=(), held_as=jnp.bfloat16):
    values = jax.random.normal(key, dims, jnp.float32) * spread
    if len(shards) > 0:
        values = block_scale(key, dims, shards, -0.22, 0.18) * values
    return jnp.clip(values, min=-reach, max=reach).astype(held_as)


def setup_inputs(seed: int = 0, part: int = 0) -> dict:
    arg_keys = jax.random.split(jax.random.key(seed), 6)
    own_keys = jax.random.split(jax.random.fold_in(arg_keys[5], part), 6)
    return {
        "wake": draw_wake(jax.random.fold_in(jax.random.fold_in(arg_keys[5], part), 71), part),
        "release": draw_release(jax.random.fold_in(jax.random.fold_in(arg_keys[5], part), 71), part),
        "strength": gaussian(own_keys[2], (PSI, ROTORS * BLADES * TRAILERS), 1.0, 6.0, ((0, 16),), jnp.float32),
        "source_list": draw_source_list(jax.random.fold_in(jax.random.fold_in(arg_keys[5], part), 71), part),
        "list_count": draw_list_count(jax.random.fold_in(jax.random.fold_in(arg_keys[5], part), 71), part),
    }


core_square = 0.01

def segments(coords, strength):
    following = jnp.concatenate([coords[:, :, 1:, :], coords[:, :, -1:, :]], axis=2)
    middles = 0.5 * (coords + following)
    levers = (following - coords) * (strength[None, :, None, :] * (0.25 / math.pi))
    return (middles, levers)

def induce(points, middles, levers, active):
    delta_one = points[0][:, None, :, None] - middles[0][:, :, None, :]
    delta_two = points[1][:, None, :, None] - middles[1][:, :, None, :]
    delta_three = points[2][:, None, :, None] - middles[2][:, :, None, :]
    inverse = lax.rsqrt(delta_one * delta_one + delta_two * delta_two + delta_three * delta_three + core_square)
    weight = inverse * inverse * inverse * active[:, :, None, None]
    lever_one = levers[0][:, :, None, :]
    lever_two = levers[1][:, :, None, :]
    lever_three = levers[2][:, :, None, :]
    swirl_one = lax.optimization_barrier(jnp.sum((lever_two * delta_three - lever_three * delta_two) * weight, axis=(1, 3)))
    swirl_two = lax.optimization_barrier(jnp.sum((lever_three * delta_one - lever_one * delta_three) * weight, axis=(1, 3)))
    swirl_three = lax.optimization_barrier(jnp.sum((lever_one * delta_two - lever_two * delta_one) * weight, axis=(1, 3)))
    return jnp.stack([swirl_one, swirl_two, swirl_three])

def velocity(coords, strength, source_list, list_count):
    middles, levers = segments(coords, strength)
    tile_count = coords.shape[1] * coords.shape[2]
    flat_mid = middles.reshape(3, tile_count, 128)
    flat_lever = levers.reshape(3, tile_count, 128)
    blocks = tile_count // 8
    slot_count = source_list.shape[2]
    targets = coords.reshape(3, blocks, 8, 128).transpose(1, 0, 2, 3)
    indices = source_list.reshape(blocks, 8, slot_count)
    active = (jnp.arange(slot_count, dtype=jnp.int32)[None, None, :] < list_count.reshape(blocks, 8)[:, :, None]).astype(jnp.float32)

    def one_block(packed):
        points, picked, weights = packed
        chosen_mid = jnp.take(flat_mid, picked.reshape(-1), axis=1).reshape(3, 8, slot_count, 128)
        chosen_lever = jnp.take(flat_lever, picked.reshape(-1), axis=1).reshape(3, 8, slot_count, 128)
        return induce(points, chosen_mid, chosen_lever, weights)
    swirling = lax.map(one_block, (targets, indices, active))
    swirling = swirling.transpose(1, 0, 2, 3).reshape(coords.shape)
    drift = jnp.array([0.0, 0.0, -0.2], dtype=jnp.float32)[:, None, None, None]
    return swirling + drift

def backward(coords, boundary):
    rolled = jnp.roll(coords, 1, axis=1)
    return jnp.concatenate([boundary[:, :, None, :], rolled[:, :, :-1, :]], axis=2)

def reference(wake, release, strength, source_list, list_count):
    positions = wake
    induced = jnp.zeros_like(wake)
    for sweep_index in range(SWEEPS):
        speed_now = velocity(positions, strength, source_list, list_count)
        back_pos = backward(positions, release)
        back_speed = backward(speed_now, jnp.zeros_like(release))
        predicted = back_pos + 0.05 * back_speed
        induced = velocity(predicted, strength, source_list, list_count)
        corrected = back_pos + 0.025 * (back_speed + induced)
        positions = positions + 0.5 * (corrected - positions)
    return (positions, induced)
```

```python
import functools
import math

import jax
import jax.numpy as jnp
from jax import lax
from jax.experimental import pallas as pl
from jax.experimental.pallas import tpu as pltpu
from jax.sharding import PartitionSpec as P

SWEEPS = 2
STEP = 0.05
core_square = 0.01
NODES = 128
GROUP = 4
MESH = pl.DeviceIdType.MESH


def split_three(value):
    first = value.astype(jnp.bfloat16).astype(jnp.float32)
    rest = value - first
    second = rest.astype(jnp.bfloat16).astype(jnp.float32)
    return first, second, rest - second


def velocity_of(
    ages,
    slots,
    blocks,
    centre,
    picked,
    raw_target,
    raw_source,
    raw_lever,
    target_tab,
    source_tab,
    lever_tab,
    sum_tab,
    result_tab,
):
    zeros = jnp.zeros((ages, NODES), jnp.float32)
    ones = jnp.ones((ages, NODES), jnp.float32)
    row = lax.broadcasted_iota(jnp.int32, (ages, NODES), 0)

    def rows_of(tile, k):
        return pl.ds(tile * 8 + k, ages, stride=8)

    for k in range(5, 8):
        raw_target[rows_of(0, k), :] = zeros
        for block in range(blocks):
            raw_source[rows_of(block * ages, k), :] = zeros
    raw_target[rows_of(0, 3), :] = ones
    for block in range(blocks):
        raw_source[rows_of(block * ages, 4), :] = ones
        for k in range(6, 8):
            raw_lever[rows_of(block * ages, k), :] = zeros
    source_tab[blocks * ages] = jnp.zeros(source_tab.shape[1:], jnp.bfloat16)
    lever_tab[blocks * ages] = jnp.zeros(lever_tab.shape[1:], jnp.bfloat16)

    def velocity(fields, strengths, target):
        moved = [target[c] - centre[c] for c in range(3)]
        for c in range(3):
            raw_target[rows_of(0, c), :] = moved[c]
        raw_target[rows_of(0, 4), :] = (
            moved[0] * moved[0] + moved[1] * moved[1] + moved[2] * moved[2]
        )
        for block in range(blocks):
            coords = [fields[block][c] - centre[c] for c in range(3)]
            following = [
                jnp.where(row == ages - 1, q, pltpu.roll(q, ages - 1, 0)) for q in coords
            ]
            gain = strengths[block] * (0.25 / math.pi)
            mid = [0.5 * (q + f) for q, f in zip(coords, following)]
            lev = [(f - q) * gain for q, f in zip(coords, following)]
            base = block * ages
            for c in range(3):
                raw_source[rows_of(base, c), :] = -2.0 * mid[c]
                raw_lever[rows_of(base, c), :] = lev[c]
                d, e = (c + 1) % 3, (c + 2) % 3
                raw_lever[rows_of(base, 3 + c), :] = lev[d] * mid[e] - lev[e] * mid[d]
            raw_source[rows_of(base, 3), :] = (
                mid[0] * mid[0] + mid[1] * mid[1] + mid[2] * mid[2] + core_square
            )

        def prepare_sources(tile):
            at = pl.ds(pl.multiple_of(tile * 8, 8), 8)
            one, two, three = split_three(raw_source[at, :])
            source_tab[tile] = jnp.concatenate(
                [one, two, three, one, two, one], axis=0
            ).astype(jnp.bfloat16)
            one, two, three = split_three(raw_lever[at, :])
            lever_tab[tile] = jnp.concatenate(
                [one, two, three, jnp.zeros_like(one)], axis=0
            ).astype(jnp.bfloat16)

        def prepare_targets(tile):
            at = pl.ds(pl.multiple_of(tile * 8, 8), 8)
            one, two, three = split_three(raw_target[at, :])
            pile = jnp.concatenate(
                [one, one, one, two, two, three, jnp.zeros((NODES - 48, NODES), jnp.float32)],
                axis=0,
            )
            target_tab[tile] = pile.T.astype(jnp.bfloat16)

        def prepare(i, carry):
            for u in range(8):
                prepare_sources(i * 8 + u)
            return carry

        def prepare_both(i, carry):
            for u in range(4):
                prepare_targets(i * 4 + u)
            return prepare(i, carry)

        lax.fori_loop(0, ages // 4, prepare_both, 0)
        if blocks > 2:
            lax.fori_loop(ages // 4, blocks * ages // 8, prepare, 0)

        def one_tile(tile):
            total = None
            left = target_tab[tile][:, :48]
            for slot in range(0, slots, 2):
                first, second = picked(tile, slot), picked(tile, slot + 1)
                right = jnp.concatenate([source_tab[first], source_tab[second]], axis=1)
                square = jnp.dot(left, right, preferred_element_type=jnp.float32)
                inverse = lax.rsqrt(jnp.maximum(square, core_square))
                weight = inverse * inverse * inverse
                high = weight.astype(jnp.bfloat16)
                low = (weight - high.astype(jnp.float32)).astype(jnp.bfloat16)
                levers = jnp.concatenate([lever_tab[first], lever_tab[second]], axis=1)
                term = lax.dot_general(
                    jnp.concatenate([high, low], axis=0),
                    levers,
                    (((1,), (1,)), ((), ())),
                    preferred_element_type=jnp.float32,
                )
                total = term if total is None else total + term
            sum_tab[tile, :, :32] = total[:NODES] + total[NODES:]

        def tiles(i, carry):
            for u in range(GROUP):
                one_tile(i * GROUP + u)
            return carry

        lax.fori_loop(0, ages // GROUP, tiles, 0)

        def finish(i, carry):
            for u in range(4):
                tile = i * 4 + u
                flat = sum_tab[tile].T
                at = pl.ds(pl.multiple_of(tile * 8, 8), 8)
                result_tab[at, :] = flat[0:8] + flat[8:16] + flat[16:24]
            return carry

        lax.fori_loop(0, ages // 4, finish, 0)
        total = [result_tab[rows_of(0, k), :] for k in range(6)]
        swirl = []
        for c in range(3):
            d, e = (c + 1) % 3, (c + 2) % 3
            swirl.append(total[d] * moved[e] - total[e] * moved[d] - total[3 + c])
        swirl[2] = swirl[2] - 0.2
        return swirl

    sum_tab[...] = jnp.zeros_like(sum_tab)
    return velocity


def table_shapes(ages, blocks):
    f32, bf16 = jnp.float32, jnp.bfloat16
    return [
        pltpu.VMEM((ages * 8, NODES), f32),
        pltpu.VMEM((blocks * ages * 8, NODES), f32),
        pltpu.VMEM((blocks * ages * 8, NODES), f32),
        pltpu.VMEM((ages, NODES, NODES), bf16),
        pltpu.VMEM((blocks * ages + 1, 48, NODES), bf16),
        pltpu.VMEM((blocks * ages + 1, 32, NODES), bf16),
        pltpu.VMEM((ages, NODES, NODES), f32),
        pltpu.VMEM((ages * 8, NODES), f32),
    ]


def relax_kernel(
    device_count,
    ages,
    slots,
    wake_ref,
    release_ref,
    strength_ref,
    list_ref,
    count_ref,
    relaxed_ref,
    induced_ref,
    own_ref,
    got_ref,
    edge_ref,
    edge_strength_ref,
    pred_ref,
    send_sem,
    recv_sem,
    edge_send,
    edge_recv,
    *tables,
):
    me = lax.axis_index("azim")
    cases = lax.axis_index("cases")

    def ahead(distance):
        return (cases, lax.rem(me + distance + device_count, device_count))

    barrier = pltpu.get_barrier_semaphore()
    for distance in (1, 2, -1, -2):
        pl.semaphore_signal(barrier, inc=1, device_id=ahead(distance), device_id_type=MESH)
    pl.semaphore_wait(barrier, 4)

    def send(round_index, source):
        copies = [
            pltpu.make_async_remote_copy(
                src_ref=source,
                dst_ref=got_ref.at[round_index, hop],
                send_sem=send_sem.at[round_index, hop],
                recv_sem=recv_sem.at[round_index, hop],
                device_id=ahead(hop + 1),
                device_id_type=MESH,
            )
            for hop in range(2)
        ]
        for copy in copies:
            copy.start()
        return copies

    edges = [
        pltpu.make_async_remote_copy(
            src_ref=source,
            dst_ref=target,
            send_sem=edge_send.at[i],
            recv_sem=edge_recv.at[i],
            device_id=ahead(1),
            device_id_type=MESH,
        )
        for i, (source, target) in enumerate(
            ((release_ref, edge_ref), (strength_ref, edge_strength_ref))
        )
    ]
    own_ref[0] = wake_ref[:, 0]
    pending = send(0, own_ref.at[0])
    for copy in edges:
        copy.start()

    row = lax.broadcasted_iota(jnp.int32, (ages, NODES), 0)
    centre = [jnp.sum(wake_ref[c, 0]) * (1.0 / (ages * NODES)) for c in range(3)]

    def picked(tile, slot):
        ident = list_ref[0, tile, slot]
        column = ident // ages
        local = jnp.where(column == me, 0, ages) + ident % ages
        return jnp.where(slot < count_ref[0, tile], local, 2 * ages)

    velocity = velocity_of(ages, slots, 2, centre, picked, *tables)

    def back(field, edge):
        return jnp.where(row == 0, edge, pltpu.roll(field, 1, 0))

    def receive(copies):
        for copy in copies:
            copy.wait()

    strength_own = strength_ref[...]
    receive(pending)
    for copy in edges:
        copy.wait()
    strengths = (strength_own, edge_strength_ref[...])

    for sweep in range(SWEEPS):
        at_pos, at_speed = 2 * sweep, 2 * sweep + 1
        position = [own_ref[at_pos, c] for c in range(3)]
        behind = [got_ref[at_pos, 0, c] for c in range(3)]
        speed = velocity((position, behind), strengths, position)
        for c in range(3):
            own_ref[at_speed, c] = speed[c]
        receive(send(at_speed, own_ref.at[at_speed]))
        for block in range(2):
            for c in range(3):
                edge = release_ref[c] if block == 0 else edge_ref[c]
                pred_ref[block, c] = back(got_ref[at_pos, block, c], edge) + STEP * back(
                    got_ref[at_speed, block, c], 0.0
                )
        predicted = [[pred_ref[block, c] for c in range(3)] for block in range(2)]
        induced = velocity(predicted, strengths, predicted[0])
        for c in range(3):
            back_pos = back(got_ref[at_pos, 0, c], release_ref[c])
            back_speed = back(got_ref[at_speed, 0, c], 0.0)
            corrected = back_pos + 0.5 * STEP * (back_speed + induced[c])
            old = own_ref[at_pos, c]
            new = old + 0.5 * (corrected - old)
            if sweep == SWEEPS - 1:
                relaxed_ref[c, 0] = new
                induced_ref[c, 0] = induced[c]
            else:
                own_ref[at_pos + 2, c] = new
        if sweep < SWEEPS - 1:
            receive(send(at_pos + 2, own_ref.at[at_pos + 2]))


def relax_near(device_count, wake, release, strength, source_list, list_count):
    ages, slots = wake.shape[2], source_list.shape[2]
    rounds = 2 * SWEEPS
    f32 = jnp.float32
    vmem = pl.BlockSpec(memory_space=pltpu.VMEM)
    smem = pl.BlockSpec(memory_space=pltpu.SMEM)
    field = (3, ages, NODES)
    return pl.pallas_call(
        functools.partial(relax_kernel, device_count, ages, slots),
        out_shape=(
            jax.ShapeDtypeStruct(wake.shape, f32),
            jax.ShapeDtypeStruct(wake.shape, f32),
        ),
        in_specs=[vmem, vmem, vmem, smem, smem],
        out_specs=(vmem, vmem),
        scratch_shapes=[
            pltpu.VMEM((rounds,) + field, f32),
            pltpu.VMEM((rounds, 2) + field, f32),
            pltpu.VMEM(release.shape, f32),
            pltpu.VMEM(strength.shape, f32),
            pltpu.VMEM((2,) + field, f32),
            pltpu.SemaphoreType.DMA((rounds, 2)),
            pltpu.SemaphoreType.DMA((rounds, 2)),
            pltpu.SemaphoreType.DMA((2,)),
            pltpu.SemaphoreType.DMA((2,)),
            *table_shapes(ages, 2),
        ],
        compiler_params=pltpu.CompilerParams(
            collective_id=0, has_side_effects=True, vmem_limit_bytes=32 * 2**20
        ),
    )(wake, release, strength, source_list, list_count)


def induce_kernel(ages, slots, blocks, target_ref, window_ref, strength_ref, pick_ref, out_ref, *tables):
    centre = [jnp.sum(target_ref[c, 0]) * (1.0 / (ages * NODES)) for c in range(3)]
    velocity = velocity_of(
        ages, slots, blocks, centre, lambda tile, slot: pick_ref[tile * slots + slot], *tables
    )
    fields = [[window_ref[c, block] for c in range(3)] for block in range(blocks)]
    strengths = [strength_ref[block : block + 1, :] for block in range(blocks)]
    target = [target_ref[c, 0] for c in range(3)]
    for c, part in enumerate(velocity(fields, strengths, target)):
        out_ref[c, 0] = part


def induce_window(coords, window, window_strength, picks, slots):
    ages, blocks = coords.shape[2], window.shape[1]
    vmem = pl.BlockSpec(memory_space=pltpu.VMEM)
    return pl.pallas_call(
        functools.partial(induce_kernel, ages, slots, blocks),
        out_shape=jax.ShapeDtypeStruct(coords.shape, jnp.float32),
        in_specs=[vmem, vmem, vmem, pl.BlockSpec(memory_space=pltpu.SMEM)],
        out_specs=vmem,
        scratch_shapes=table_shapes(ages, blocks),
        compiler_params=pltpu.CompilerParams(vmem_limit_bytes=48 * 2**20),
    )(coords, window, window_strength, picks)


def shifted(block, axis, distance):
    devices = range(lax.axis_size(axis))
    route = [((i - distance) % len(devices), i) for i in devices]
    return lax.ppermute(block, axis, route)


def shift_local(coords, edge_pos, boundary):
    rolled = jnp.concatenate([edge_pos, coords[:, :-1]], axis=1)
    return jnp.concatenate([boundary[:, :, None, :], rolled[:, :, :-1, :]], axis=2)


def gather_window(coords, strength, reach_blocks):
    psi_local = coords.shape[1]
    if reach_blocks > 1:
        first_block = shifted((coords, strength), "azim", -(reach_blocks - 1))
    else:
        first_block = (coords, strength)
    width_cols = 2 * reach_blocks * psi_local
    pos_buffer = jnp.zeros((3, width_cols) + coords.shape[2:], jnp.float32)
    str_buffer = jnp.zeros((width_cols, strength.shape[1]), jnp.float32)
    pos_buffer = lax.dynamic_update_slice_in_dim(pos_buffer, first_block[0], 0, axis=1)
    str_buffer = lax.dynamic_update_slice_in_dim(str_buffer, first_block[1], 0, axis=0)

    def advance(hop_index, carry):
        current, pos_now, str_now = carry
        current = shifted((current[0], current[1]), "azim", 1)
        pos_now = lax.dynamic_update_slice_in_dim(
            pos_now, current[0], hop_index * psi_local, axis=1
        )
        str_now = lax.dynamic_update_slice_in_dim(
            str_now, current[1], hop_index * psi_local, axis=0
        )
        return (current, pos_now, str_now)

    result = lax.fori_loop(1, 2 * reach_blocks, advance, (first_block, pos_buffer, str_buffer))
    return (result[1], result[2])


def on_device(wake, release, strength, source_list, list_count):
    device_count = lax.axis_size("azim")
    reach_blocks = device_count // 16
    if reach_blocks == 1 and wake.shape[1] == 1:
        return relax_near(device_count, wake, release, strength, source_list, list_count)
    own_index = lax.axis_index("azim")
    psi_local = wake.shape[1]
    age_count = wake.shape[2]
    slot_count = source_list.shape[2]
    column = source_list // age_count
    age_part = source_list % age_count
    owner_block = column // psi_local
    within = column % psi_local
    offset = (owner_block - own_index + reach_blocks) % device_count - reach_blocks
    local_ids = ((reach_blocks - 1 - offset) * psi_local + within) * age_count + age_part
    used = jnp.arange(slot_count, dtype=jnp.int32) < list_count[:, :, None]
    empty = 2 * reach_blocks * psi_local * age_count
    picks = jnp.where(used, local_ids, empty).reshape(-1)

    def velocity(coords):
        win_pos, win_str = gather_window(coords, strength, reach_blocks)
        return induce_window(coords, win_pos, win_str, picks, slot_count)

    positions = wake
    induced = jnp.zeros_like(wake)
    for sweep_index in range(SWEEPS):
        speed_now = velocity(positions)
        edge_pos, edge_speed = shifted((positions, speed_now), "azim", 1)
        back_pos = shift_local(positions, edge_pos, release)
        back_speed = shift_local(speed_now, edge_speed, jnp.zeros_like(release))
        predicted = back_pos + 0.05 * back_speed
        induced = velocity(predicted)
        corrected = back_pos + 0.025 * (back_speed + induced)
        positions = positions + 0.5 * (corrected - positions)
    return (positions, induced)


def solution(mesh):
    placed = (
        P(None, ("cases", "azim"), None, None),
        P(None, ("cases", "azim"), None),
        P(("cases", "azim"), None),
        P(("cases", "azim"), None, None),
        P(("cases", "azim"), None),
    )
    return jax.shard_map(
        on_device,
        mesh=mesh,
        in_specs=placed,
        out_specs=(P(None, ("cases", "azim"), None, None), P(None, ("cases", "azim"), None, None)),
        check_vma=False,
    )
```
